32 devices in a mesh: op: 8 (over y, x, core), sector: 4 (over z).
Axes of the slice: x: 2, y: 2, z: 4, core: 2. Of those that a mesh axis runs over, the one named last changes fastest.
Arguments:
- wavefunction: bfloat16 [8, 512, 512], P('sector'), may hold values from -10 to 10
- left_blocks: bfloat16 [32, 8, 512, 512], P('op', 'sector'), may hold values from -1 to 1
- right_blocks: bfloat16 [32, 8, 512, 512], P('op', 'sector'), may hold values from -1 to 1
- target_sector: int32 [32, 8], P('op', 'sector'), may hold values from 0 to 7, as said below
- preconditioner: float32 [8, 512, 512], P('sector', 'op'), may hold values from 1 to 10
Outputs:
- sigma_first: float32 [8, 512, 512], P('sector', 'op')
- sigma_second: float32 [8, 512, 512], P('sector', 'op')
The draws below stay inside these ranges and needn't reach their ends.
Inputs may be any that keep to these rules, and one draw needn't show every extreme that they name: `target_sector`: sector t belongs to index t // 2 of sector. Among the 4 x 2 pairs (k, s) that one device holds, at most 3 have targets belonging to one index of sector, and on every device some index of sector gets exactly 3.
All inputs are finite; a program needn't handle non-finite values.
Results may differ from the reference program's by a relative error of at most 0.0034.
Values may be sent and summed in bfloat16 or wider, within the bound.
A program may use at most 64 MiB of HBM per device.

```python
import math
import jax
import jax.numpy as jnp
from jax import lax

BLOCK = 512
SEC_DEV = 2
TERM_DEV = 4
NSEC = 8
TERMS = 32


def device_owners(key, favourite):
    owner_count = NSEC // SEC_DEV
    task_count = TERM_DEV * SEC_DEV
    limit = (task_count + owner_count - 1) // owner_count + 1
    pick_key, hot_key, perm_key, order_key = jax.random.split(key, 4)
    random_hot = jax.random.randint(hot_key, (), 0, owner_count)
    use_fav = jax.random.randint(pick_key, (), 0, 2)
    hot_owner = jnp.where(use_fav == 1, favourite, random_hot)
    others = (hot_owner + 1 + jnp.arange((owner_count - 1) * limit) // limit) % owner_count
    others = jax.random.permutation(perm_key, others)
    owners = jnp.concatenate([jnp.full((limit,), hot_owner, jnp.int32), others[:task_count - limit].astype(jnp.int32)])
    return jax.random.permutation(order_key, owners)


def draw_target_sector(key, part):
    owner_count = NSEC // SEC_DEV
    op_count = TERMS // TERM_DEV
    device_count = op_count * owner_count
    fav_key, dev_key, low_key = jax.random.split(jax.random.fold_in(key, 7), 3)
    favourite = jax.random.randint(fav_key, (), 0, owner_count)
    keys = jax.random.split(dev_key, device_count)
    owners = jax.vmap(lambda single: device_owners(single, favourite))(keys)
    low = jax.random.randint(low_key, owners.shape, 0, SEC_DEV)
    targets = owners * SEC_DEV + low
    targets = targets.reshape(op_count, owner_count, TERM_DEV, SEC_DEV)
    targets = jnp.transpose(targets, (0, 2, 1, 3)).reshape(TERMS, NSEC)
    return targets.astype(jnp.int32)


def draw_wavefunction(key, part):
    own_key = jax.random.fold_in(key, 11)
    position = jnp.arange(BLOCK, dtype=jnp.float32) / (BLOCK - 1)
    values = jnp.clip(jax.random.normal(own_key, (NSEC, BLOCK, BLOCK), jnp.float32), -4.0, 4.0)
    scales = 2.5 ** position
    return (values * scales[None, :, None]).astype(jnp.bfloat16)


def operator_draw(key, spread, diagonal):
    shape = (TERMS, NSEC, BLOCK, BLOCK)
    values = jnp.clip(jax.random.normal(key, shape, jnp.float32), -3.0, 3.0)
    identity = jnp.eye(BLOCK, dtype=jnp.float32)
    return (values * spread + diagonal * identity[None, None]).astype(jnp.bfloat16)


def draw_left_blocks(key, part):
    own_key = jax.random.fold_in(key, 23)
    spread = 1.0 / (BLOCK * TERMS) ** 0.5
    return operator_draw(own_key, spread, 0.5 / TERMS ** 0.5)


def draw_right_blocks(key, part):
    own_key = jax.random.fold_in(key, 29)
    spread = 1.0 / BLOCK ** 0.5
    return operator_draw(own_key, spread, 0.5)


def levels(rng, dims, cuts, low, largest):
    factor_of, own = 1.0, jax.random.fold_in(rng, 6)
    for axis_at, blocks in cuts:
        steps = jnp.exp(jax.random.uniform(jax.random.fold_in(own, axis_at), (blocks,), jnp.float32, low / len(cuts), largest / len(cuts)))
        factor_of = factor_of * jnp.repeat(steps, dims[axis_at] // blocks).reshape([-1 if axis == axis_at else 1 for axis in range(len(dims))])
    return factor_of


def setup_inputs(seed: int = 0) -> dict:
    seeds = jax.random.split(jax.random.key(seed), 6)
    wavefunction = draw_wavefunction(jax.random.fold_in(seeds[5], 71), 0)
    left_blocks = draw_left_blocks(jax.random.fold_in(seeds[5], 71), 0)
    right_blocks = draw_right_blocks(jax.random.fold_in(seeds[5], 71), 0)
    target_sector = draw_target_sector(jax.random.fold_in(seeds[5], 71), 0)
    preconditioner = jnp.clip(jnp.exp(math.log(10.0) - 2.3025851 * jax.random.uniform(seeds[4], (NSEC, BLOCK, BLOCK), jnp.float32) ** levels(seeds[4], (NSEC, BLOCK, BLOCK), ((0, 4), (1, 8)), -0.2, 0.2)), 1.0, 10.0)
    return dict(wavefunction=wavefunction, left_blocks=left_blocks, right_blocks=right_blocks, target_sector=target_sector, preconditioner=preconditioner)


def apply_terms(left_blocks, right_blocks, target_sector, vector):
    term_count, sector_count = target_sector.shape
    block_width = vector.shape[1]

    def one_task(task_index, totals):
        term_index = task_index // sector_count
        sector_index = task_index % sector_count
        middle = jnp.dot(left_blocks[term_index, sector_index], vector[sector_index], preferred_element_type=jnp.float32).astype(jnp.bfloat16)
        contribution = lax.dot_general(middle, right_blocks[term_index, sector_index], (((1,), (1,)), ((), ())), preferred_element_type=jnp.float32)
        target = target_sector[term_index, sector_index]
        return totals.at[target].add(contribution)
    initial = jnp.zeros((sector_count, block_width, block_width), jnp.float32)
    return lax.fori_loop(0, term_count * sector_count, one_task, initial)

def reference(wavefunction, left_blocks, right_blocks, target_sector, preconditioner):
    sigma_first = apply_terms(left_blocks, right_blocks, target_sector, wavefunction)
    floats = wavefunction.astype(jnp.float32)
    norm_sq = jnp.sum(floats * floats)
    rayleigh = jnp.sum(floats * sigma_first) / norm_sq
    correction = (sigma_first - (rayleigh - 1.0) * floats) / preconditioner
    update = correction - jnp.sum(floats * correction) / norm_sq * floats
    new_vector = (update * jnp.sqrt(norm_sq) * lax.rsqrt(jnp.sum(update * update) + 1e-06)).astype(jnp.bfloat16)
    sigma_second = apply_terms(left_blocks, right_blocks, target_sector, new_vector)
    return (sigma_first, sigma_second)
```

```python
import functools

import jax
import jax.numpy as jnp
from jax import lax
from jax.experimental import pallas as pl
from jax.experimental.pallas import tpu as pltpu
from jax.sharding import PartitionSpec as P

MESH = pl.DeviceIdType.MESH
LANES = 128
HEAD = 16
TOP = 32000.0


def kernel(dims, wave, left, right, target, pre, out1, out2, *scratch):
    op_n, sec_n, terms, parts, width, rows, cap = dims
    stages = op_n.bit_length() - 1
    groups = width // LANES
    tasks = terms * parts
    orders = []
    for a in range(parts):
        order = list(range(stages))
        if a % 2:
            for b in range(1, stages - 1, 2):
                order[b], order[b + 1] = order[b + 1], order[b]
        orders.append(order)
    lv, rv, mid, cbuf, acc, vec, gath, red1, red2 = scratch[:9]
    smsg = scratch[9:9 + stages]
    rmsg = scratch[9 + stages:9 + 2 * stages]
    (zs, zr, load_sem, ssem, rsem, zssem, zrsem, gssem, grsem, p_s, p_r, q_s, q_r) = scratch[9 + 2 * stages:]

    me = lax.axis_index("op")
    zed = lax.axis_index("sector")

    def flip(b):
        bit = (me // (1 << b)) % 2
        return me + (1 - 2 * bit) * (1 << b)

    def row_block(order, pos):
        total = 0
        for k, b in enumerate(order):
            bit = ((me // (1 << b)) % 2 + (pos // (1 << (stages - 1 - k))) % 2) % 2
            total = total + bit * (1 << b)
        return total

    def owner(i):
        return lax.rem(zed + 1 + i, sec_n)

    loads = []
    for i in range(tasks):
        loads.append(pltpu.make_async_copy(left.at[i // parts, i % parts], lv.at[i], load_sem.at[0, i]))
    for i in range(tasks):
        loads.append(pltpu.make_async_copy(right.at[i // parts, i % parts], rv.at[i], load_sem.at[1, i]))
    for c in loads:
        c.start()

    barrier = pltpu.get_barrier_semaphore()
    for d in range(1, op_n):
        pl.semaphore_signal(barrier, inc=1, device_id=(lax.rem(me + d, op_n), zed), device_id_type=MESH)
    for d in range(1, sec_n):
        pl.semaphore_signal(barrier, inc=1, device_id=(me, lax.rem(zed + d, sec_n)), device_id_type=MESH)

    def encode(dst, src, first, count, peak):
        top = jnp.maximum(jnp.full((HEAD, LANES), jnp.max(peak), jnp.float32), 1e-30)
        power = jnp.ceil(jnp.log2(top))
        dst[pl.ds(0, HEAD), :] = power.astype(jnp.int32).astype(jnp.int16)
        scale = (jnp.exp2(-power) * TOP)[:1, :]

        def one(p, carry):
            for g in range(groups):
                x = src[first + p, :, pl.ds(g * LANES, LANES)]
                coded = jnp.round(x * scale).astype(jnp.int32).astype(jnp.int16)
                dst[pl.ds(pl.multiple_of(HEAD + (p * groups + g) * rows, 16), rows), :] = coded
            return carry

        lax.fori_loop(0, count, one, 0)

    def step_of(src):
        power = src[pl.ds(0, HEAD), :].astype(jnp.int32).astype(jnp.float32)
        return (jnp.exp2(power) * (1.0 / TOP))[:1, :]

    def decode(src, step, p, g):
        part = src[pl.ds(pl.multiple_of(HEAD + (p * groups + g) * rows, 16), rows), :]
        return part.astype(jnp.int32).astype(jnp.float32) * step

    def stage_copy(i, a, k):
        return pltpu.make_async_remote_copy(
            src_ref=smsg[k].at[i, a], dst_ref=rmsg[k].at[i, a],
            send_sem=ssem.at[i, a, k], recv_sem=rsem.at[i, a, k],
            device_id=(flip(orders[a][k]), zed), device_id_type=MESH)

    def z_copy(i, a):
        return pltpu.make_async_remote_copy(
            src_ref=zs.at[i, a], dst_ref=zr.at[i, a],
            send_sem=zssem.at[i, a], recv_sem=zrsem.at[i, a],
            device_id=(me, owner(i)), device_id_type=MESH)

    def middles(source, first):
        for i in range(tasks):
            if first:
                loads[i].wait()
            mid[i] = jnp.dot(lv[i], source[i % parts], preferred_element_type=jnp.float32).astype(jnp.bfloat16)
        if first:
            for i in range(tasks):
                loads[tasks + i].wait()

    def products(i):
        q = owner(i)
        count = jnp.int32(0)
        index = [jnp.int32(0)] * cap
        weight = [[jnp.float32(0)] * cap for _ in range(parts)]
        for task in range(tasks):
            t = target[task // parts, task % parts]
            mine = t // parts == q
            for j in range(cap):
                hit = jnp.logical_and(mine, count == j)
                index[j] = jnp.where(hit, task, index[j])
                for a in range(parts):
                    here = jnp.logical_and(hit, t % parts == a)
                    weight[a][j] = jnp.where(here, 1.0, weight[a][j])
            count = count + mine.astype(jnp.int32)
        for j in range(cap):
            cbuf[j] = lax.dot_general(mid[index[j]], rv[index[j]], (((1,), (1,)), ((), ())),
                                      preferred_element_type=jnp.float32)
        return weight

    def first_send(i, weight):
        half = op_n // 2
        for a in range(parts):
            def one(p, peak):
                at = pl.multiple_of(row_block(orders[a], p) * rows, rows)
                for g in range(groups):
                    cols = pl.ds(g * LANES, LANES)
                    x = cbuf[0, pl.ds(at, rows), cols] * weight[a][0]
                    for j in range(1, cap):
                        x = x + cbuf[j, pl.ds(at, rows), cols] * weight[a][j]
                    acc[i, a, p, :, cols] = x
                    peak = jnp.maximum(peak, jnp.abs(x))
                return peak

            zero = jnp.zeros((rows, LANES), jnp.float32)
            peak = lax.fori_loop(half, op_n, one, zero)
            encode(smsg[0].at[i, a], acc.at[i, a], half, half, peak)
            stage_copy(i, a, 0).start()
            lax.fori_loop(0, half, one, zero)

    def absorb(i, a, k):
        stage_copy(i, a, k).wait_recv()
        src = rmsg[k].at[i, a]
        step = step_of(src)
        have = op_n >> (k + 1)

        def one(p, peak):
            for g in range(groups):
                cols = pl.ds(g * LANES, LANES)
                x = acc[i, a, p, :, cols] + decode(src, step, p, g)
                acc[i, a, p, :, cols] = x
                peak = jnp.maximum(peak, jnp.abs(x))
            return peak

        zero = jnp.zeros((rows, LANES), jnp.float32)
        if k + 1 < stages:
            half = have // 2
            peak = lax.fori_loop(half, have, one, zero)
            encode(smsg[k + 1].at[i, a], acc.at[i, a], half, half, peak)
            stage_copy(i, a, k + 1).start()
            lax.fori_loop(0, half, one, zero)
        else:
            peak = one(0, zero)
            if i < sec_n - 1:
                encode(zs.at[i, a], acc.at[i, a], 0, 1, peak)
                z_copy(i, a).start()

    def apply(source, out, first):
        middles(source, first)
        for tau in range(sec_n + stages):
            if tau < sec_n:
                weight = products(tau)
                if first and tau == 0:
                    pl.semaphore_wait(barrier, op_n - 1 + sec_n - 1)
                first_send(tau, weight)
            for k in range(stages):
                i = tau - 1 - k
                if 0 <= i < sec_n:
                    for a in range(parts):
                        absorb(i, a, k)
        for a in range(parts):
            steps = []
            for i in range(sec_n - 1):
                z_copy(i, a).wait_recv()
                steps.append(step_of(zr.at[i, a]))
            for g in range(groups):
                cols = pl.ds(g * LANES, LANES)
                x = acc[sec_n - 1, a, 0, :, cols]
                for i in range(sec_n - 1):
                    x = x + decode(zr.at[i, a], steps[i], 0, g)
                out[a, :, cols] = x
        for i in range(sec_n):
            for a in range(parts):
                for k in range(stages):
                    stage_copy(i, a, k).wait_send()
                if i < sec_n - 1:
                    z_copy(i, a).wait_send()

    apply(wave, out1, True)

    own = pl.ds(pl.multiple_of(me * rows, rows), rows)
    sums = [jnp.zeros((rows, LANES), jnp.float32)] * 7
    for a in range(parts):
        for g in range(groups):
            cols = pl.ds(g * LANES, LANES)
            w = wave[a, own, cols].astype(jnp.float32)
            s = out1[a, :, cols]
            inv = 1.0 / pre[a, :, cols]
            ua, ub = s * inv, w * inv
            for n, x in enumerate((w * w, w * s, w * ua, w * ub, ua * ua, ua * ub, ub * ub)):
                sums[n] = sums[n] + x
    tile = jnp.concatenate([jnp.sum(x, axis=0, keepdims=True) for x in sums]
                           + [jnp.zeros((1, LANES), jnp.float32)], axis=0)
    red1[me] = tile

    def p_copy(d, slot):
        return pltpu.make_async_remote_copy(
            src_ref=red1.at[me], dst_ref=red1.at[slot], send_sem=p_s.at[d], recv_sem=p_r.at[d],
            device_id=(lax.rem(me + d, op_n), zed), device_id_type=MESH)

    for d in range(1, op_n):
        p_copy(d, me).start()
    for d in range(1, op_n):
        p_copy(d, lax.rem(me + op_n - d, op_n)).wait_recv()
    total = red1[0]
    for d in range(1, op_n):
        total = total + red1[d]
    red2[zed] = total

    def q_copy(d, slot):
        return pltpu.make_async_remote_copy(
            src_ref=red2.at[zed], dst_ref=red2.at[slot], send_sem=q_s.at[d], recv_sem=q_r.at[d],
            device_id=(me, lax.rem(zed + d, sec_n)), device_id_type=MESH)

    for d in range(1, sec_n):
        q_copy(d, zed).start()
    for d in range(1, sec_n):
        q_copy(d, lax.rem(zed + sec_n - d, sec_n)).wait_recv()
    total = red2[0]
    for d in range(1, sec_n):
        total = total + red2[d]
    flat = jnp.broadcast_to(jnp.sum(total, axis=1, keepdims=True), (8, LANES))
    norm_sq, corr, wa, wb, aa, ab, bb = [flat[n:n + 1, :] for n in range(7)]
    shift = corr / norm_sq - 1.0
    projected = wa - shift * wb
    correction_sq = aa - 2.0 * shift * ab + shift * shift * bb
    along = projected / norm_sq
    update_sq = jnp.maximum(correction_sq - projected * along, 0.0)
    scale = jnp.sqrt(norm_sq) * lax.rsqrt(update_sq + 1e-06)
    for a in range(parts):
        for g in range(groups):
            cols = pl.ds(g * LANES, LANES)
            w = wave[a, own, cols].astype(jnp.float32)
            correction = (out1[a, :, cols] - shift * w) / pre[a, :, cols]
            gath[a, 0, :, cols] = ((correction - along * w) * scale).astype(jnp.bfloat16)

    def g_copy(a, k):
        n = op_n >> (k + 1)
        return pltpu.make_async_remote_copy(
            src_ref=gath.at[a, pl.ds(0, n)], dst_ref=gath.at[a, pl.ds(n, n)],
            send_sem=gssem.at[a, k], recv_sem=grsem.at[a, k],
            device_id=(flip(orders[a][k]), zed), device_id_type=MESH)

    for k in reversed(range(stages)):
        for a in range(parts):
            g_copy(a, k).start()
        for a in range(parts):
            g_copy(a, k).wait_recv()
    for a in range(parts):
        def place(p, carry):
            at = pl.multiple_of(row_block(orders[a], p) * rows, rows)
            vec[a, pl.ds(at, rows), :] = gath[a, p]
            return carry
        lax.fori_loop(0, op_n, place, 0)
    for d in range(1, op_n):
        p_copy(d, me).wait_send()
    for d in range(1, sec_n):
        q_copy(d, zed).wait_send()
    for k in range(stages):
        for a in range(parts):
            g_copy(a, k).wait_send()

    apply(vec, out2, False)


def on_device(op_n, sec_n, wave, left, right, target, pre):
    terms, parts = target.shape
    width = wave.shape[1]
    rows = pre.shape[1]
    tasks = terms * parts
    cap = (tasks + sec_n - 1) // sec_n + 1
    stages = op_n.bit_length() - 1
    groups = width // LANES
    dims = (op_n, sec_n, terms, parts, width, rows, cap)
    vm = pltpu.VMEM
    f32, b16, i16 = jnp.float32, jnp.bfloat16, jnp.int16
    messages = [vm((sec_n, parts, HEAD + (op_n >> (k + 1)) * groups * rows, LANES), i16) for k in range(stages)]
    zmsg = vm((sec_n - 1, parts, HEAD + groups * rows, LANES), i16)
    dma = pltpu.SemaphoreType.DMA
    scratch = [
        vm((tasks, width, width), b16), vm((tasks, width, width), b16), vm((tasks, width, width), b16),
        vm((cap, width, width), f32), vm((sec_n, parts, op_n, rows, width), f32),
        vm((parts, width, width), b16), vm((parts, op_n, rows, width), b16),
        vm((op_n, 8, LANES), f32), vm((sec_n, 8, LANES), f32),
        *messages, *messages, zmsg, zmsg,
        dma((2, tasks)), dma((sec_n, parts, stages)), dma((sec_n, parts, stages)),
        dma((sec_n - 1, parts)), dma((sec_n - 1, parts)),
        dma((parts, stages)), dma((parts, stages)),
        dma((op_n,)), dma((op_n,)), dma((sec_n,)), dma((sec_n,)),
    ]
    whole = pl.BlockSpec(memory_space=pltpu.VMEM)
    anywhere = pl.BlockSpec(memory_space=pl.ANY)
    flops = 2 * 2 * 2 * tasks * width ** 3
    out = jax.ShapeDtypeStruct((parts, rows, width), f32)
    return pl.pallas_call(
        functools.partial(kernel, dims),
        out_shape=(out, out),
        in_specs=[whole, anywhere, anywhere, pl.BlockSpec(memory_space=pltpu.SMEM), whole],
        out_specs=(whole, whole),
        scratch_shapes=scratch,
        compiler_params=pltpu.CompilerParams(
            collective_id=0, has_side_effects=True, vmem_limit_bytes=56 * 1024 * 1024),
        cost_estimate=pl.CostEstimate(flops=flops, bytes_accessed=4 * tasks * width * width, transcendentals=0),
    )(wave, left, right, target, pre)


def solution(mesh):
    placed = (
        P("sector", None, None),
        P("op", "sector", None, None),
        P("op", "sector", None, None),
        P("op", "sector"),
        P("sector", "op", None),
    )
    return jax.shard_map(
        functools.partial(on_device, mesh.shape["op"], mesh.shape["sector"]),
        mesh=mesh,
        in_specs=placed,
        out_specs=(P("sector", "op", None), P("sector", "op", None)),
        check_vma=False,
    )
```

```python
import functools

import jax
import jax.numpy as jnp
from jax import lax
from jax.experimental import pallas as pl
from jax.experimental.pallas import tpu as pltpu
from jax.sharding import PartitionSpec as P

MESH = pl.DeviceIdType.MESH
LANES = 128
HEAD = 16
TOP = 32000.0


def kernel(dims, wave, left, right, target, pre, out1, out2, *scratch):
    op_n, sec_n, terms, parts, width, rows, cap = dims
    stages = op_n.bit_length() - 1
    groups = width // LANES
    tasks = terms * parts
    orders = []
    for a in range(parts):
        order = list(range(stages))
        if a % 2:
            for b in range(1, stages - 1, 2):
                order[b], order[b + 1] = order[b + 1], order[b]
        orders.append(order)
    lv, rv, mid, cbuf, acc, vec, gath, red1, red2 = scratch[:9]
    smsg = scratch[9:9 + stages]
    rmsg = scratch[9 + stages:9 + 2 * stages]
    (zs, zr, load_sem, ssem, rsem, zssem, zrsem, gssem, grsem, p_s, p_r, q_s, q_r) = scratch[9 + 2 * stages:]

    me = lax.axis_index("op")
    zed = lax.axis_index("sector")

    def flip(b):
        bit = (me // (1 << b)) % 2
        return me + (1 - 2 * bit) * (1 << b)

    def row_block(order, pos):
        total = 0
        for k, b in enumerate(order):
            bit = ((me // (1 << b)) % 2 + (pos // (1 << (stages - 1 - k))) % 2) % 2
            total = total + bit * (1 << b)
        return total

    def owner(i):
        return lax.rem(zed + 1 + i, sec_n)

    loads = []
    for i in range(tasks):
        loads.append(pltpu.make_async_copy(left.at[i // parts, i % parts], lv.at[i], load_sem.at[0, i]))
    for i in range(tasks):
        loads.append(pltpu.make_async_copy(right.at[i // parts, i % parts], rv.at[i], load_sem.at[1, i]))
    for c in loads:
        c.start()

    barrier = pltpu.get_barrier_semaphore()
    for d in range(1, op_n):
        pl.semaphore_signal(barrier, inc=1, device_id=(lax.rem(me + d, op_n), zed), device_id_type=MESH)
    for d in range(1, sec_n):
        pl.semaphore_signal(barrier, inc=1, device_id=(me, lax.rem(zed + d, sec_n)), device_id_type=MESH)

    def header(dst, bound):
        power = jnp.ceil(jnp.log2(bound))
        dst[pl.ds(0, HEAD), :] = power.astype(jnp.int32).astype(jnp.int16)
        return (jnp.exp2(-power) * TOP)[:1, :]

    def put(dst, scale, p, g, x):
        coded = jnp.round(x * scale).astype(jnp.int32).astype(jnp.int16)
        dst[pl.ds(pl.multiple_of(HEAD + (p * groups + g) * rows, 16), rows), :] = coded

    def reach(src):
        return jnp.exp2(src[pl.ds(0, HEAD), :].astype(jnp.int32).astype(jnp.float32))

    def step_of(src):
        return (reach(src) * (1.0 / TOP))[:1, :]

    def decode(src, step, p, g):
        part = src[pl.ds(pl.multiple_of(HEAD + (p * groups + g) * rows, 16), rows), :]
        return part.astype(jnp.int32).astype(jnp.float32) * step

    def stage_copy(i, a, k):
        return pltpu.make_async_remote_copy(
            src_ref=smsg[k].at[i, a], dst_ref=rmsg[k].at[i, a],
            send_sem=ssem.at[i, a, k], recv_sem=rsem.at[i, a, k],
            device_id=(flip(orders[a][k]), zed), device_id_type=MESH)

    def z_copy(i, a):
        return pltpu.make_async_remote_copy(
            src_ref=zs.at[i, a], dst_ref=zr.at[i, a],
            send_sem=zssem.at[i, a], recv_sem=zrsem.at[i, a],
            device_id=(me, owner(i)), device_id_type=MESH)

    def products(i, source):
        q = owner(i)
        count = jnp.int32(0)
        index = [jnp.int32(0)] * cap
        weight = [[jnp.float32(0)] * cap for _ in range(parts)]
        for task in range(tasks):
            t = target[task % parts, task // parts]
            mine = t // parts == q
            for j in range(cap):
                hit = jnp.logical_and(mine, count == j)
                index[j] = jnp.where(hit, task, index[j])
                for a in range(parts):
                    here = jnp.logical_and(hit, t % parts == a)
                    weight[a][j] = jnp.where(here, 1.0, weight[a][j])
            count = count + mine.astype(jnp.int32)
        for j in range(cap):
            mid[j] = jnp.dot(lv[index[j]], source[index[j] % parts],
                             preferred_element_type=jnp.float32).astype(jnp.bfloat16)
        for j in range(cap):
            cbuf[j] = lax.dot_general(mid[j], rv[index[j]], (((1,), (1,)), ((), ())),
                                      preferred_element_type=jnp.float32)
        return weight

    def first_send(i, weight, bounds):
        half = op_n // 2
        zero = jnp.zeros((rows, LANES), jnp.float32)
        for a in range(parts):
            def one(p, peak):
                at = pl.multiple_of(row_block(orders[a], p) * rows, rows)
                for g in range(groups):
                    cols = pl.ds(g * LANES, LANES)
                    x = cbuf[0, pl.ds(at, rows), cols] * weight[a][0]
                    for j in range(1, cap):
                        x = x + cbuf[j, pl.ds(at, rows), cols] * weight[a][j]
                    acc[i, a, p, :, cols] = x
                    peak = jnp.maximum(peak, jnp.abs(x))
                return peak

            peak = lax.fori_loop(half, op_n, one, zero)
            top = jnp.maximum(jnp.full((HEAD, LANES), jnp.max(peak), jnp.float32), 1e-30)
            dst = smsg[0].at[i, a]
            scale = header(dst, top)

            def code(p, carry):
                for g in range(groups):
                    put(dst, scale, p, g, acc[i, a, half + p, :, pl.ds(g * LANES, LANES)])
                return carry

            lax.fori_loop(0, half, code, 0)
            stage_copy(i, a, 0).start()
            peak = lax.fori_loop(0, half, one, zero)
            bounds[i, a] = jnp.maximum(jnp.full((HEAD, LANES), jnp.max(peak), jnp.float32), 1e-30)

    def absorb(i, a, k, bounds):
        stage_copy(i, a, k).wait_recv()
        src = rmsg[k].at[i, a]
        step = step_of(src)
        bounds[i, a] = bounds[i, a] + reach(src)
        have = op_n >> (k + 1)
        last = k + 1 == stages

        def add(p, carry):
            for g in range(groups):
                cols = pl.ds(g * LANES, LANES)
                acc[i, a, p, :, cols] = acc[i, a, p, :, cols] + decode(src, step, p, g)
            return carry

        if last and i == sec_n - 1:
            add(0, 0)
            return
        half = 0 if last else have // 2
        dst = zs.at[i, a] if last else smsg[k + 1].at[i, a]
        scale = header(dst, bounds[i, a])

        def pass_on(p, carry):
            for g in range(groups):
                x = acc[i, a, half + p, :, pl.ds(g * LANES, LANES)] + decode(src, step, half + p, g)
                put(dst, scale, p, g, x)
            return carry

        if last:
            pass_on(0, 0)
            z_copy(i, a).start()
        else:
            lax.fori_loop(0, half, pass_on, 0)
            stage_copy(i, a, k + 1).start()
            lax.fori_loop(0, half, add, 0)

    def apply(source, out, first):
        bounds = {}
        if first:
            for c in loads:
                c.wait()
        for tau in range(sec_n + stages):
            if tau < sec_n:
                weight = products(tau, source)
            for k in range(stages):
                i = tau - 1 - k
                if k == stages - 1 and tau < sec_n:
                    if first and tau == 0:
                        pl.semaphore_wait(barrier, op_n - 1 + sec_n - 1)
                    first_send(tau, weight, bounds)
                if 0 <= i < sec_n:
                    for a in range(parts):
                        absorb(i, a, k, bounds)
        for a in range(parts):
            steps = []
            for i in range(sec_n - 1):
                z_copy(i, a).wait_recv()
                steps.append(step_of(zr.at[i, a]))
            for g in range(groups):
                cols = pl.ds(g * LANES, LANES)
                x = acc[sec_n - 1, a, 0, :, cols]
                for i in range(sec_n - 1):
                    x = x + decode(zr.at[i, a], steps[i], 0, g)
                out[a, :, cols] = x
        for i in range(sec_n):
            for a in range(parts):
                for k in range(stages):
                    stage_copy(i, a, k).wait_send()
                if i < sec_n - 1:
                    z_copy(i, a).wait_send()

    apply(wave, out1, True)

    own = pl.ds(pl.multiple_of(me * rows, rows), rows)
    sums = [jnp.zeros((rows, LANES), jnp.float32)] * 7
    for a in range(parts):
        for g in range(groups):
            cols = pl.ds(g * LANES, LANES)
            w = wave[a, own, cols].astype(jnp.float32)
            s = out1[a, :, cols]
            inv = 1.0 / pre[a, :, cols]
            ua, ub = s * inv, w * inv
            for n, x in enumerate((w * w, w * s, w * ua, w * ub, ua * ua, ua * ub, ub * ub)):
                sums[n] = sums[n] + x
    tile = jnp.concatenate([jnp.sum(x, axis=0, keepdims=True) for x in sums]
                           + [jnp.zeros((1, LANES), jnp.float32)], axis=0)
    red1[me] = tile

    def p_copy(d, slot):
        return pltpu.make_async_remote_copy(
            src_ref=red1.at[me], dst_ref=red1.at[slot], send_sem=p_s.at[d], recv_sem=p_r.at[d],
            device_id=(lax.rem(me + d, op_n), zed), device_id_type=MESH)

    for d in range(1, op_n):
        p_copy(d, me).start()
    for d in range(1, op_n):
        p_copy(d, lax.rem(me + op_n - d, op_n)).wait_recv()
    total = red1[0]
    for d in range(1, op_n):
        total = total + red1[d]
    red2[zed] = total

    def q_copy(d, slot):
        return pltpu.make_async_remote_copy(
            src_ref=red2.at[zed], dst_ref=red2.at[slot], send_sem=q_s.at[d], recv_sem=q_r.at[d],
            device_id=(me, lax.rem(zed + d, sec_n)), device_id_type=MESH)

    for d in range(1, sec_n):
        q_copy(d, zed).start()
    for d in range(1, sec_n):
        q_copy(d, lax.rem(zed + sec_n - d, sec_n)).wait_recv()
    total = red2[0]
    for d in range(1, sec_n):
        total = total + red2[d]
    flat = jnp.broadcast_to(jnp.sum(total, axis=1, keepdims=True), (8, LANES))
    norm_sq, corr, wa, wb, aa, ab, bb = [flat[n:n + 1, :] for n in range(7)]
    shift = corr / norm_sq - 1.0
    projected = wa - shift * wb
    correction_sq = aa - 2.0 * shift * ab + shift * shift * bb
    along = projected / norm_sq
    update_sq = jnp.maximum(correction_sq - projected * along, 0.0)
    scale = jnp.sqrt(norm_sq) * lax.rsqrt(update_sq + 1e-06)
    for a in range(parts):
        for g in range(groups):
            cols = pl.ds(g * LANES, LANES)
            w = wave[a, own, cols].astype(jnp.float32)
            correction = (out1[a, :, cols] - shift * w) / pre[a, :, cols]
            gath[a, 0, :, cols] = ((correction - along * w) * scale).astype(jnp.bfloat16)

    def g_copy(a, k, m):
        n = op_n >> (k + 1)
        lo, size = (0, 1) if m == 0 else (1 << (m - 1), 1 << (m - 1))
        return pltpu.make_async_remote_copy(
            src_ref=gath.at[a, pl.ds(lo, size)], dst_ref=gath.at[a, pl.ds(n + lo, size)],
            send_sem=gssem.at[a, k, m], recv_sem=grsem.at[a, k, m],
            device_id=(flip(orders[a][k]), zed), device_id_type=MESH)

    for k in reversed(range(stages)):
        for a in range(parts):
            g_copy(a, k, 0).start()
    for k in reversed(range(stages)):
        for m in range(stages - k):
            for a in range(parts):
                g_copy(a, k, m).wait_recv()
        for later in reversed(range(k)):
            for a in range(parts):
                g_copy(a, later, stages - k).start()
    for a in range(parts):
        def place(p, carry):
            at = pl.multiple_of(row_block(orders[a], p) * rows, rows)
            vec[a, pl.ds(at, rows), :] = gath[a, p]
            return carry
        lax.fori_loop(0, op_n, place, 0)
    for d in range(1, op_n):
        p_copy(d, me).wait_send()
    for d in range(1, sec_n):
        q_copy(d, zed).wait_send()
    for k in range(stages):
        for a in range(parts):
            for m in range(stages - k):
                g_copy(a, k, m).wait_send()

    apply(vec, out2, False)


def on_device(op_n, sec_n, wave, left, right, target, pre):
    terms, parts = target.shape
    width = wave.shape[1]
    rows = pre.shape[1]
    tasks = terms * parts
    cap = (tasks + sec_n - 1) // sec_n + 1
    stages = op_n.bit_length() - 1
    groups = width // LANES
    dims = (op_n, sec_n, terms, parts, width, rows, cap)
    vm = pltpu.VMEM
    f32, b16, i16 = jnp.float32, jnp.bfloat16, jnp.int16
    messages = [vm((sec_n, parts, HEAD + (op_n >> (k + 1)) * groups * rows, LANES), i16) for k in range(stages)]
    zmsg = vm((sec_n - 1, parts, HEAD + groups * rows, LANES), i16)
    dma = pltpu.SemaphoreType.DMA
    scratch = [
        vm((tasks, width, width), b16), vm((tasks, width, width), b16), vm((cap, width, width), b16),
        vm((cap, width, width), f32), vm((sec_n, parts, op_n, rows, width), f32),
        vm((parts, width, width), b16), vm((parts, op_n, rows, width), b16),
        vm((op_n, 8, LANES), f32), vm((sec_n, 8, LANES), f32),
        *messages, *messages, zmsg, zmsg,
        dma((2, tasks)), dma((sec_n, parts, stages)), dma((sec_n, parts, stages)),
        dma((sec_n - 1, parts)), dma((sec_n - 1, parts)),
        dma((parts, stages, stages)), dma((parts, stages, stages)),
        dma((op_n,)), dma((op_n,)), dma((sec_n,)), dma((sec_n,)),
    ]
    whole = pl.BlockSpec(memory_space=pltpu.VMEM)
    anywhere = pl.BlockSpec(memory_space=pl.ANY)
    flops = 2 * 2 * 2 * tasks * width ** 3
    out = jax.ShapeDtypeStruct((parts, rows, width), f32)
    return pl.pallas_call(
        functools.partial(kernel, dims),
        out_shape=(out, out),
        in_specs=[whole, anywhere, anywhere, pl.BlockSpec(memory_space=pltpu.SMEM), whole],
        out_specs=(whole, whole),
        scratch_shapes=scratch,
        compiler_params=pltpu.CompilerParams(
            collective_id=0, has_side_effects=True, vmem_limit_bytes=61 * 1024 * 1024),
        cost_estimate=pl.CostEstimate(flops=flops, bytes_accessed=4 * tasks * width * width, transcendentals=0),
    )(wave, left, right, target.T, pre)


def solution(mesh):
    placed = (
        P("sector", None, None),
        P("op", "sector", None, None),
        P("op", "sector", None, None),
        P("op", "sector"),
        P("sector", "op", None),
    )
    return jax.shard_map(
        functools.partial(on_device, mesh.shape["op"], mesh.shape["sector"]),
        mesh=mesh,
        in_specs=placed,
        out_specs=(P("sector", "op", None), P("sector", "op", None)),
        check_vma=False,
    )
```
